512 devices in a mesh: blk: 64 (over z_hi, x, y), uly: 8 (over z_lo, core).
Axes of the slice: x: 4, y: 8, z: 8 (z_hi: 2, z_lo: 4; z = z_hi * 4 + z_lo), core: 2. Of those that a mesh axis runs over, the one named last changes fastest.
Arguments:
- queries: bfloat16 [16384, 4096], P(('blk', 'uly')), may hold values from -40 to 40
- keys: bfloat16 [16384, 4096], P(('blk', 'uly')), may hold values from -40 to 40
- values: bfloat16 [16384, 4096], P(('blk', 'uly')), may hold values from -6 to 6
- flags: int32 [16384], P(('blk', 'uly')), may hold values from 0 to 1
- q_mask: bfloat16 [4096], replicated, may hold values from -15 to 15
- k_mask: bfloat16 [4096], replicated, may hold values from -6 to 6
- v_mask: bfloat16 [4096], replicated, may hold values from -6 to 6
Outputs:
- attended: bfloat16 [16384, 4096], P(('blk', 'uly'))
The draws below stay inside these ranges and needn't reach their ends.
All inputs are finite; a program needn't handle non-finite values.
Results may differ from the reference program's by a relative error of at most 0.0082.
Values may be sent and summed in bfloat16 or wider, within the bound.
A program may use at most 64 MiB of HBM per device.

```python
import math
import jax
import jax.numpy as jnp
from jax import lax

HEADS = 32
HD = 128
LENGTH = 2048
SEQS = 8
TOKENS = 16384


def shared_rows(key):
    row_key = jax.random.fold_in(key, 11)
    seq_pick = jnp.arange(6, dtype=jnp.int32) * SEQS // 6
    offsets = jax.random.randint(row_key, (6,), 0, LENGTH - 1).astype(jnp.int32)
    anchors = (seq_pick * LENGTH + offsets).astype(jnp.int32)
    return anchors


def anchor_hits(anchors, offset):
    positions = jnp.arange(TOKENS, dtype=jnp.int32)
    return positions[:, None] == anchors[None, :] + offset


def draw_flags(key, part):
    anchors = shared_rows(key)
    key = jax.random.fold_in(key, 3)
    coins = jax.random.randint(key, (TOKENS,), 0, 2).astype(jnp.int32)
    touched = jnp.any(anchor_hits(anchors, 0) | anchor_hits(anchors, 1), axis=1)
    return jnp.where(touched, 0, coins).astype(jnp.int32)


def draw_queries(key, part):
    key = jax.random.fold_in(key, 1)
    base = jnp.clip(jax.random.normal(key, (TOKENS, HEADS * HD), jnp.float32) * 2.5, -15.0, 15.0)
    return base.astype(jnp.bfloat16)


def draw_keys(key, part):
    key = jax.random.fold_in(key, 2)
    base = jnp.clip(jax.random.normal(key, (TOKENS, HEADS * HD), jnp.float32), -6.0, 6.0)
    return base.astype(jnp.bfloat16)


def shard_levels(stream_key, shape, shards, low, largest):
    level, own = 1.0, jax.random.fold_in(stream_key, 6)
    for axis_at, parts in shards:
        heights = jnp.exp(jax.random.uniform(jax.random.fold_in(own, axis_at), (parts,), jnp.float32, low / len(shards), largest / len(shards)))
        level = level * jnp.repeat(heights, shape[axis_at] // parts).reshape([-1 if axis == axis_at else 1 for axis in range(len(shape))])
    return level


def scatter_about(rng, shape, scale, most, cuts=(), kind=jnp.bfloat16):
    drawn = jax.random.normal(rng, shape, jnp.float32) * scale
    if len(cuts) > 0:
        drawn = shard_levels(rng, shape, cuts, -0.22, 0.18) * drawn
    return jnp.clip(drawn, min=-most, max=most).astype(kind)


def setup_inputs(seed: int = 0) -> dict:
    key_of = jax.random.split(jax.random.key(seed), 8)
    queries = draw_queries(jax.random.fold_in(key_of[7], 71), 0)
    keys = draw_keys(jax.random.fold_in(key_of[7], 71), 0)
    values = scatter_about(key_of[2], (TOKENS, HEADS * HD), 1.0, 6.0, ((0, 512),))
    flags = draw_flags(jax.random.fold_in(key_of[7], 71), 0)
    q_mask = scatter_about(key_of[4], (HEADS * HD,), 2.5, 15.0)
    k_mask = scatter_about(key_of[5], (HEADS * HD,), 1.0, 6.0)
    v_mask = scatter_about(key_of[6], (HEADS * HD,), 1.0, 6.0)
    return {"queries": queries, "keys": keys, "values": values, "flags": flags, "q_mask": q_mask, "k_mask": k_mask, "v_mask": v_mask}


rope_base = 500000.0

def rotate_heads(hidden_rows, positions):
    row_count = hidden_rows.shape[0]
    half_dim = HD // 2
    split_rows = hidden_rows.astype(jnp.float32).reshape(row_count, -1, HD)
    freq_index = jnp.arange(half_dim).astype(jnp.float32)
    frequency = jnp.exp(freq_index * (-2.0 * math.log(rope_base) / HD))
    angles = positions[:, None] * frequency[None, :]
    cosine = jnp.cos(angles)[:, None, :]
    sine_part = jnp.sin(angles)[:, None, :]
    first_half = split_rows[..., :half_dim]
    second_half = split_rows[..., half_dim:]
    rotated = jnp.concatenate([first_half * cosine - second_half * sine_part, second_half * cosine + first_half * sine_part], axis=-1)
    return rotated.reshape(row_count, -1).astype(jnp.bfloat16)

def attend_sequence(operands):
    seq_queries, seq_keys, seq_values, seq_flags, q_mask, k_mask, v_mask = operands
    masked = (seq_flags == 1)[:, None]
    query_in = jnp.where(masked, q_mask[None, :], seq_queries)
    key_in = jnp.where(masked, k_mask[None, :], seq_keys)
    value_in = jnp.where(masked, v_mask[None, :], seq_values)
    positions = jnp.arange(LENGTH).astype(jnp.float32)
    query_rot = rotate_heads(query_in, positions)
    key_rot = rotate_heads(key_in, positions)
    query_heads = query_rot.reshape(LENGTH, HEADS, HD).transpose(1, 0, 2)
    key_heads = key_rot.reshape(LENGTH, HEADS, HD).transpose(1, 0, 2)
    value_heads = value_in.reshape(LENGTH, HEADS, HD).transpose(1, 0, 2)
    block_rows = math.gcd(LENGTH, 1024)
    score_scale = 1.0 / math.sqrt(HD)

    def one_head(head_operands):
        head_query, head_key, head_value = head_operands
        query_blocks = head_query.reshape(LENGTH // block_rows, block_rows, HD)

        def one_block(query_block):
            scores = jnp.dot(query_block, head_key.T, preferred_element_type=jnp.float32) * score_scale
            row_top = lax.optimization_barrier(jnp.max(scores, axis=1, keepdims=True))
            weights = jnp.exp(scores - row_top)
            weight_sum = lax.optimization_barrier(jnp.sum(weights, axis=1, keepdims=True))
            mixture = jnp.dot(weights.astype(jnp.bfloat16), head_value, preferred_element_type=jnp.float32)
            return (mixture / weight_sum).astype(jnp.bfloat16)
        return lax.map(one_block, query_blocks).reshape(LENGTH, HD)
    attended = lax.map(one_head, (query_heads, key_heads, value_heads))
    return attended.transpose(1, 0, 2).reshape(LENGTH, HEADS * HD)

def reference(queries, keys, values, flags, q_mask, k_mask, v_mask):
    width = HEADS * HD
    seq_queries = queries.reshape(SEQS, LENGTH, width)
    seq_keys = keys.reshape(SEQS, LENGTH, width)
    seq_values = values.reshape(SEQS, LENGTH, width)
    seq_flags = flags.reshape(SEQS, LENGTH)

    def per_sequence(operands):
        sq, sk, sv, sf = operands
        return attend_sequence((sq, sk, sv, sf, q_mask, k_mask, v_mask))
    attended = lax.map(per_sequence, (seq_queries, seq_keys, seq_values, seq_flags))
    return attended.reshape(TOKENS, width)
```

```python
import functools
import math

import jax
import jax.numpy as jnp
import numpy as np
from jax import lax
from jax.experimental import pallas as pl
from jax.experimental.pallas import tpu as pltpu
from jax.sharding import PartitionSpec as P

HD = 128
ROPE_BASE = 500000.0
NY, NZ = 8, 4
CHIPS = NY * NZ
MESH = pl.DeviceIdType.MESH
SCALE = math.log2(math.e) / math.sqrt(HD)


def kernel(rows, q_hbm, k_hbm, v_hbm, flags_hbm, qm_hbm, km_hbm, vm_hbm, freq_hbm, out_ref,
           q_in, k_in, v_in, flags_ref, qm_ref, km_ref, vm_ref, freq_ref, masks, kv_stage, q_stage, kv_buf, q_buf, o_stage, o_buf,
           in_sem, kv_send, q_send, fwd_send, o_send, kv_recv, q_recv, fwd_recv, o_recv):
    blk, uly = lax.axis_index("blk"), lax.axis_index("uly")
    blk0, y, z, core = blk // NY * NY, blk % NY, uly // 2, uly % 2
    here = y * NZ + z
    sibling = (blk, z * 2 + 1 - core)
    half = CHIPS * rows
    own_slot = (NY - 1) * NZ

    def device(chip):
        return (blk0 + chip // NZ, chip % NZ * 2 + core)

    def kv_dy(i):
        j = i // NZ
        return (j // 2 + 1) * (1 - 2 * (j % 2)) * (1 - j // (NY - 1))

    def q_dy(i):
        j = i // NZ
        return (NY // 2 - (j + 1) // 2) * (1 - 2 * (j % 2))

    def ahead(dy, dz):
        return (y + dy + NY) % NY * NZ + (z + dz) % NZ

    def behind(dy, dz):
        return (y - dy + NY) % NY * NZ + (z - dz + NZ) % NZ

    barrier = pltpu.get_barrier_semaphore()

    def greet(i, carry):
        pl.semaphore_signal(barrier, inc=1, device_id=device((here + i) % CHIPS), device_id_type=MESH)
        return carry

    lax.fori_loop(1, CHIPS, greet, 0)
    pl.semaphore_signal(barrier, inc=1, device_id=sibling, device_id_type=MESH)

    loads = [
        pltpu.make_async_copy(src, dst, in_sem.at[i])
        for i, (src, dst) in enumerate((
            (freq_hbm, freq_ref), (flags_hbm, flags_ref), (qm_hbm, qm_ref), (km_hbm, km_ref), (vm_hbm, vm_ref),
            (k_hbm, k_in), (v_hbm, v_in), (q_hbm, q_in),
        ))
    ]
    for load in loads:
        load.start()
    for load in loads[:5]:
        load.wait()

    row = lax.broadcasted_iota(jnp.int32, (rows, HD), 0)
    lane = lax.broadcasted_iota(jnp.int32, (rows, HD), 1)
    position = ((y * (NZ * 2) + uly) * rows + row).astype(jnp.float32)
    angle = position * freq_ref[...]
    cosine = jnp.cos(angle)
    sine = jnp.where(lane < HD // 2, -jnp.sin(angle), jnp.sin(angle))
    diagonal = lax.broadcasted_iota(jnp.int32, (rows, rows), 0) == lax.broadcasted_iota(jnp.int32, (rows, rows), 1)
    flag_column = jnp.sum(
        jnp.where(diagonal, flags_ref[...].astype(jnp.float32), 0.0), axis=1, keepdims=True
    )
    masked = jnp.broadcast_to(flag_column, (rows, HD)) == 1.0

    for i, m_ref in enumerate((qm_ref, km_ref, vm_ref)):
        masks[i] = m_ref[...].astype(jnp.float32)

    def picked(x_in, which, chip):
        x = x_in[:, pl.ds(pl.multiple_of(chip * HD, HD), HD)].astype(jnp.float32)
        return jnp.where(masked, masks[which, pl.ds(chip, 1), :], x)

    def rotated(x):
        return (x * cosine + pltpu.roll(x, HD // 2, 1) * sine).astype(jnp.bfloat16)

    loads[5].wait()
    loads[6].wait()

    def prepare_kv(chip, carry):
        kv_stage[chip, 0] = rotated(picked(k_in, 1, chip))
        kv_stage[chip, 1] = picked(v_in, 2, chip).astype(jnp.bfloat16)
        return carry

    lax.fori_loop(0, CHIPS, prepare_kv, 0)
    loads[7].wait()

    def prepare_q(chip, carry):
        q_stage[chip] = rotated(picked(q_in, 0, chip))
        return carry

    lax.fori_loop(0, CHIPS, prepare_q, 0)

    pl.semaphore_wait(barrier, CHIPS)

    def slot(i):
        return pl.ds(pl.multiple_of(i * rows, rows), rows)

    per_kv, per_q = CHIPS // 4, CHIPS // 4

    def send_kv(i, carry):
        chip = ahead(kv_dy(i), i % NZ)
        pltpu.make_async_remote_copy(
            kv_stage.at[chip], kv_buf.at[:, slot(i)], kv_send, kv_recv.at[i // per_kv],
            device_id=device(chip), device_id_type=MESH,
        ).start()
        return carry

    lax.fori_loop(0, own_slot, send_kv, 0)
    pltpu.make_async_copy(kv_stage.at[here], kv_buf.at[:, slot(own_slot)], kv_recv.at[own_slot // per_kv]).start()
    lax.fori_loop(own_slot + 1, CHIPS, send_kv, 0)

    def send_q(i, carry):
        chip = ahead(q_dy(i), i % NZ)
        pltpu.make_async_remote_copy(
            q_stage.at[chip], q_buf.at[slot(i)], q_send, q_recv.at[i // per_q],
            device_id=device(chip), device_id_type=MESH,
        ).start()
        return carry

    lax.fori_loop(0, own_slot, send_q, 0)
    pltpu.make_async_copy(q_stage.at[here], q_buf.at[slot(own_slot)], q_recv.at[own_slot // per_q]).start()
    lax.fori_loop(own_slot + 1, CHIPS, send_q, 0)

    def drain(ref, sem):
        pltpu.make_async_copy(ref, ref, sem).wait()

    kv_rows = per_kv * rows
    for g in range(4):
        part = pl.ds(g * kv_rows, kv_rows)
        drain(kv_buf.at[:, part], kv_recv.at[g])
        pltpu.make_async_remote_copy(
            kv_buf.at[:, part], kv_buf.at[:, pl.ds(half + g * kv_rows, kv_rows)], fwd_send, fwd_recv,
            device_id=sibling, device_id_type=MESH,
        ).start()
    drain(kv_buf.at[:, pl.ds(half, half)], fwd_recv)

    q_rows = per_q * rows

    def return_o(i, carry):
        chip = behind(q_dy(i), i % NZ)
        pltpu.make_async_remote_copy(
            o_stage.at[slot(i)], o_buf.at[here], o_send, o_recv,
            device_id=device(chip), device_id_type=MESH,
        ).start()
        return carry

    def attend(g, carry):
        part = pl.ds(pl.multiple_of(g * q_rows, q_rows), q_rows)
        drain(q_buf.at[part], q_recv.at[g])
        scores = lax.dot_general(
            q_buf[part, :], kv_buf[0], (((1,), (1,)), ((), ())), preferred_element_type=jnp.float32
        )
        top = jnp.max(scores, axis=1, keepdims=True)
        weights = jnp.exp2((scores - top) * SCALE)
        total = jnp.sum(weights, axis=1, keepdims=True)
        mixture = jnp.dot(weights.astype(jnp.bfloat16), kv_buf[1], preferred_element_type=jnp.float32)
        o_stage[part, :] = (mixture / total).astype(jnp.bfloat16)
        return carry

    def attend_and_return(g, carry):
        attend(g, carry)
        lax.fori_loop(g * per_q, (g + 1) * per_q, return_o, 0)
        return carry

    lax.fori_loop(0, 3, attend_and_return, 0)
    attend(3, 0)
    lax.fori_loop(3 * per_q, own_slot, return_o, 0)
    pltpu.make_async_copy(o_stage.at[slot(own_slot)], o_buf.at[here], o_recv).start()
    lax.fori_loop(own_slot + 1, CHIPS, return_o, 0)

    others = CHIPS - 1
    drain(kv_stage.at[pl.ds(0, others)], kv_send)
    drain(q_stage.at[pl.ds(0, others)], q_send)
    drain(kv_buf.at[:, pl.ds(0, half)], fwd_send)
    drain(o_buf, o_recv)
    for head in range(CHIPS):
        out_ref[:, head * HD:(head + 1) * HD] = o_buf[head]
    drain(o_stage.at[pl.ds(0, others * rows)], o_send)


def body(queries, keys, values, flags, q_mask, k_mask, v_mask):
    rows, width = queries.shape
    half = CHIPS * rows
    pair_lanes = np.arange(HD) % (HD // 2)
    freq = np.exp(pair_lanes * (-2.0 * math.log(ROPE_BASE) / HD)).astype(np.float32)[None, :]
    vmem = pl.BlockSpec(memory_space=pltpu.VMEM)
    hbm = pl.BlockSpec(memory_space=pltpu.HBM)
    return pl.pallas_call(
        functools.partial(kernel, rows),
        out_shape=jax.ShapeDtypeStruct((rows, width), jnp.bfloat16),
        in_specs=[hbm] * 8,
        out_specs=vmem,
        scratch_shapes=[
            pltpu.VMEM((rows, width), jnp.bfloat16),
            pltpu.VMEM((rows, width), jnp.bfloat16),
            pltpu.VMEM((rows, width), jnp.bfloat16),
            pltpu.VMEM((1, rows), jnp.int32),
            pltpu.VMEM((CHIPS, HD), jnp.bfloat16),
            pltpu.VMEM((CHIPS, HD), jnp.bfloat16),
            pltpu.VMEM((CHIPS, HD), jnp.bfloat16),
            pltpu.VMEM((1, HD), jnp.float32),
            pltpu.VMEM((3, CHIPS, HD), jnp.float32),
            pltpu.VMEM((CHIPS, 2, rows, HD), jnp.bfloat16),
            pltpu.VMEM((CHIPS, rows, HD), jnp.bfloat16),
            pltpu.VMEM((2, 2 * half, HD), jnp.bfloat16),
            pltpu.VMEM((half, HD), jnp.bfloat16),
            pltpu.VMEM((half, HD), jnp.bfloat16),
            pltpu.VMEM((CHIPS, rows, HD), jnp.bfloat16),
            pltpu.SemaphoreType.DMA((8,)),
            pltpu.SemaphoreType.DMA,
            pltpu.SemaphoreType.DMA,
            pltpu.SemaphoreType.DMA,
            pltpu.SemaphoreType.DMA,
            pltpu.SemaphoreType.DMA((4,)),
            pltpu.SemaphoreType.DMA((4,)),
            pltpu.SemaphoreType.DMA,
            pltpu.SemaphoreType.DMA,
        ],
        compiler_params=pltpu.CompilerParams(
            collective_id=0, has_side_effects=True, vmem_limit_bytes=64 * 2**20
        ),
        name="attend_plane",
    )(
        queries, keys, values, flags.reshape(1, rows),
        q_mask.reshape(CHIPS, HD), k_mask.reshape(CHIPS, HD), v_mask.reshape(CHIPS, HD), jnp.asarray(freq),
    )


def solution(mesh):
    placed = (
        P(("blk", "uly"), None),
        P(("blk", "uly"), None),
        P(("blk", "uly"), None),
        P(("blk", "uly")),
        P(),
        P(),
        P(),
    )
    return jax.shard_map(
        body, mesh=mesh, in_specs=placed, out_specs=P(("blk", "uly"), None), check_vma=False
    )
```

```python
import functools
import math

import jax
import jax.numpy as jnp
import numpy as np
from jax import lax
from jax.experimental import pallas as pl
from jax.experimental.pallas import tpu as pltpu
from jax.sharding import PartitionSpec as P

HD = 128
ROPE_BASE = 500000.0
NY, NZ = 8, 4
CHIPS = NY * NZ
MESH = pl.DeviceIdType.MESH
NEAR = (0, 1, 7, 2, 6, 3, 5, 4)
FAR = NEAR[::-1]
KV_ORDER = sorted([(dy, dz) for dy in range(NY) for dz in range(NZ)], key=lambda d: (min(d[0], NY - d[0]) + d[1], d))
Q_ORDER = sorted([(dy, dz) for dy in range(NY) for dz in range(NZ)], key=lambda d: (min(d[0], NY - d[0]) + d[1], d))
SENDS = [("kv", dy, dz) for dy, dz in KV_ORDER] + [("q", dy, dz) for dy, dz in Q_ORDER]
SCALE = math.log2(math.e) / math.sqrt(HD)


def kernel(rows, q_hbm, k_hbm, v_hbm, flags_hbm, qm_hbm, km_hbm, vm_hbm, base_hbm, step_hbm, out_ref,
           q_in, k_in, v_in, flags_ref, qm_ref, km_ref, vm_ref, base_ref, step_ref, masks, kv_stage, q_stage, kv_buf, q_buf, o_stage, o_buf,
           in_sem, kv_send, q_send, fwd_send, o_send, kv_recv, q_recv, fwd_recv, o_recv, ready):
    blk, uly = lax.axis_index("blk"), lax.axis_index("uly")
    blk0, y, z, core = blk // NY * NY, blk % NY, uly // 2, uly % 2
    here = y * NZ + z
    sibling = (blk, z * 2 + 1 - core)
    half = CHIPS * rows

    place = z * NY + y
    y_at = [y] + [jnp.where(y + d >= NY, y + d - NY, y + d) for d in range(1, NY)]
    z_at = [z, z + 1 - 2 * (z % 2), z + 2 - 4 * (z // 2), NZ - 1 - z]

    def turn_of(cy, cz):
        away = jnp.minimum(cy, NY - cy)
        late = jnp.where(cy + cz + blk0 + core == 0, 7, 0)
        return (2 * cz + away + late) * CHIPS + cz * NY + cy

    my_turn = turn_of(y, z)
    chips = [(cy, cz) for cz in range(NZ) for cy in range(NY)]
    turns = [turn_of(cy, cz) for cy, cz in chips]
    barrier = pltpu.get_barrier_semaphore()
    for (cy, cz), turn in zip(chips, turns):
        @pl.when(turn > my_turn)
        def _():
            pl.semaphore_signal(barrier, inc=1, device_id=(blk0 + cy, cz * 2 + core), device_id_type=MESH)

    @pl.when(core == 1)
    def _():
        pl.semaphore_signal(barrier, inc=1, device_id=sibling, device_id_type=MESH)

    loads = [
        pltpu.make_async_copy(src, dst, in_sem.at[i])
        for i, (src, dst) in enumerate((
            (base_hbm.at[y * (NZ * 2) + uly], base_ref), (step_hbm, step_ref), (flags_hbm, flags_ref), (qm_hbm, qm_ref), (km_hbm, km_ref), (vm_hbm, vm_ref),
            (k_hbm, k_in), (v_hbm, v_in), (q_hbm, q_in),
        ))
    ]
    for load in loads:
        load.start()

    entered = 1 - core
    for turn in turns:
        entered = entered + jnp.where(turn < my_turn, 1, 0)
    @pl.when(entered > 0)
    def _():
        pl.semaphore_wait(barrier, entered)

    for (cy, cz), turn in zip(chips, turns):
        @pl.when(turn < my_turn)
        def _():
            pl.semaphore_signal(ready.at[here], inc=1, device_id=(blk0 + cy, cz * 2 + core), device_id_type=MESH)

    @pl.when(core == 0)
    def _():
        pl.semaphore_signal(ready.at[here], inc=1, device_id=sibling, device_id_type=MESH)

    for load in loads[:6]:
        load.wait()

    lane = lax.broadcasted_iota(jnp.int32, (rows, HD), 1)
    turn, offset = base_ref[...], step_ref[...]
    cosine = turn[0:1] * offset[0] - turn[1:2] * offset[1]
    sine = turn[1:2] * offset[0] + turn[0:1] * offset[1]
    sine = jnp.where(lane < HD // 2, -sine, sine)
    diagonal = lax.broadcasted_iota(jnp.int32, (rows, rows), 0) == lax.broadcasted_iota(jnp.int32, (rows, rows), 1)
    flag_column = jnp.sum(
        jnp.where(diagonal, flags_ref[...].astype(jnp.float32), 0.0), axis=1, keepdims=True
    )
    masked = jnp.broadcast_to(flag_column, (rows, HD)) == 1.0

    for i, m_ref in enumerate((qm_ref, km_ref, vm_ref)):
        masks[i] = m_ref[...].astype(jnp.float32)

    def picked(x_in, which, chip):
        x = x_in[:, chip * HD:(chip + 1) * HD].astype(jnp.float32)
        return jnp.where(masked, masks[which, chip:chip + 1, :], x)

    def rotated(x):
        return (x * cosine + pltpu.roll(x, HD // 2, 1) * sine).astype(jnp.bfloat16)

    loads[6].wait()
    loads[7].wait()

    for chip in range(CHIPS):
        kv_stage[chip, 0] = rotated(picked(k_in, 1, chip))
        kv_stage[chip, 1] = picked(v_in, 2, chip).astype(jnp.bfloat16)
    loads[8].wait()
    for chip in range(CHIPS):
        q_stage[chip] = rotated(picked(q_in, 0, chip))

    def slot(i):
        return pl.ds(pl.multiple_of(i * rows, rows), rows)

    def peer(dy, dz):
        return y_at[dy] * NZ + z_at[dz], (blk0 + y_at[dy], z_at[dz] * 2 + core)

    def send_kv(dy, dz):
        chip, device = peer(dy, dz)
        pltpu.make_async_remote_copy(
            kv_stage.at[chip], kv_buf.at[:, slot(place)], kv_send, kv_recv.at[z],
            device_id=device, device_id_type=MESH,
        ).start()

    def send_q(dy, dz):
        chip, device = peer(dy, dz)
        if dy + dz:
            pltpu.make_async_remote_copy(
                q_stage.at[chip], q_buf.at[slot(place)], q_send, q_recv.at[z],
                device_id=device, device_id_type=MESH,
            ).start()
        else:
            pltpu.make_async_copy(q_stage.at[here], q_buf.at[slot(place)], q_recv.at[z]).start()

    pltpu.make_async_copy(kv_stage.at[here], kv_buf.at[:, slot(place)], kv_recv.at[z]).start()
    for dy, dz in KV_ORDER:
        @pl.when(turn_of(y_at[dy], z_at[dz]) < my_turn)
        def _():
            send_kv(dy, dz)

    for dy, dz in KV_ORDER:
        @pl.when(turn_of(y_at[dy], z_at[dz]) > my_turn)
        def _():
            pl.semaphore_wait(ready.at[peer(dy, dz)[0]], 1)
            send_kv(dy, dz)

    for dy, dz in Q_ORDER:
        send_q(dy, dz)

    def drain(ref, sem):
        pltpu.make_async_copy(ref, ref, sem).wait()

    group = NY * rows

    @pl.when(core == 1)
    def _():
        pl.semaphore_wait(ready.at[here], 1)

    for g in range(NZ):
        part = pl.ds(g * group, group)
        drain(kv_buf.at[:, part], kv_recv.at[g])
        pltpu.make_async_remote_copy(
            kv_buf.at[:, part], kv_buf.at[:, pl.ds(half + g * group, group)], fwd_send, fwd_recv,
            device_id=sibling, device_id_type=MESH,
        ).start()
    drain(kv_buf.at[:, pl.ds(half, half)], fwd_recv)

    for g in range(NZ):
        part = pl.ds(g * group, group)
        drain(q_buf.at[part], q_recv.at[g])
        scores = lax.dot_general(
            q_buf[part, :], kv_buf[0], (((1,), (1,)), ((), ())), preferred_element_type=jnp.float32
        )
        top = jnp.max(scores, axis=1, keepdims=True)
        weights = jnp.exp2((scores - top) * SCALE)
        total = jnp.sum(weights, axis=1, keepdims=True)
        mixture = jnp.dot(weights.astype(jnp.bfloat16), kv_buf[1], preferred_element_type=jnp.float32)
        o_stage[part, :] = (mixture / total).astype(jnp.bfloat16)
        for dy in FAR:
            back = functools.partial(
                pltpu.make_async_remote_copy, o_stage.at[slot(g * NY + y_at[dy])], o_buf.at[here], o_send, o_recv,
                device_id=(blk0 + y_at[dy], g * 2 + core), device_id_type=MESH,
            )
            if dy:
                back().start()
            else:
                @pl.when(z != g)
                def _():
                    back().start()

                @pl.when(z == g)
                def _():
                    pltpu.make_async_copy(o_stage.at[slot(place)], o_buf.at[here], o_recv).start()

    others = CHIPS - 1
    drain(kv_stage.at[pl.ds(0, others)], kv_send)
    drain(q_stage.at[pl.ds(0, others)], q_send)
    drain(kv_buf.at[:, pl.ds(0, half)], fwd_send)
    drain(o_buf, o_recv)
    for head in range(CHIPS):
        out_ref[:, head * HD:(head + 1) * HD] = o_buf[head]
    drain(o_stage.at[pl.ds(0, others * rows)], o_send)


def body(queries, keys, values, flags, q_mask, k_mask, v_mask):
    rows, width = queries.shape
    half = CHIPS * rows
    pair_lanes = np.arange(HD) % (HD // 2)
    freq = np.exp(pair_lanes * (-2.0 * math.log(ROPE_BASE) / HD)).astype(np.float32).astype(np.float64)
    base = np.arange(NY * NZ * 2)[:, None] * rows * freq
    step = np.arange(rows)[:, None] * freq
    base = np.stack([np.cos(base), np.sin(base)], axis=1).astype(np.float32)
    step = np.stack([np.cos(step), np.sin(step)]).astype(np.float32)
    vmem = pl.BlockSpec(memory_space=pltpu.VMEM)
    hbm = pl.BlockSpec(memory_space=pltpu.HBM)
    return pl.pallas_call(
        functools.partial(kernel, rows),
        out_shape=jax.ShapeDtypeStruct((rows, width), jnp.bfloat16),
        in_specs=[hbm] * 9,
        out_specs=vmem,
        scratch_shapes=[
            pltpu.VMEM((rows, width), jnp.bfloat16),
            pltpu.VMEM((rows, width), jnp.bfloat16),
            pltpu.VMEM((rows, width), jnp.bfloat16),
            pltpu.VMEM((1, rows), jnp.int32),
            pltpu.VMEM((CHIPS, HD), jnp.bfloat16),
            pltpu.VMEM((CHIPS, HD), jnp.bfloat16),
            pltpu.VMEM((CHIPS, HD), jnp.bfloat16),
            pltpu.VMEM((2, HD), jnp.float32),
            pltpu.VMEM((2, rows, HD), jnp.float32),
            pltpu.VMEM((3, CHIPS, HD), jnp.float32),
            pltpu.VMEM((CHIPS, 2, rows, HD), jnp.bfloat16),
            pltpu.VMEM((CHIPS, rows, HD), jnp.bfloat16),
            pltpu.VMEM((2, 2 * half, HD), jnp.bfloat16),
            pltpu.VMEM((half, HD), jnp.bfloat16),
            pltpu.VMEM((half, HD), jnp.bfloat16),
            pltpu.VMEM((CHIPS, rows, HD), jnp.bfloat16),
            pltpu.SemaphoreType.DMA((9,)),
            pltpu.SemaphoreType.DMA,
            pltpu.SemaphoreType.DMA,
            pltpu.SemaphoreType.DMA,
            pltpu.SemaphoreType.DMA,
            pltpu.SemaphoreType.DMA((4,)),
            pltpu.SemaphoreType.DMA((4,)),
            pltpu.SemaphoreType.DMA,
            pltpu.SemaphoreType.DMA,
            pltpu.SemaphoreType.REGULAR((CHIPS,)),
        ],
        compiler_params=pltpu.CompilerParams(
            collective_id=0, has_side_effects=True, vmem_limit_bytes=64 * 2**20
        ),
        name="attend_plane",
    )(
        queries, keys, values, flags.reshape(1, rows),
        q_mask.reshape(CHIPS, HD), k_mask.reshape(CHIPS, HD), v_mask.reshape(CHIPS, HD), jnp.asarray(base), jnp.asarray(step),
    )


def solution(mesh):
    placed = (
        P(("blk", "uly"), None),
        P(("blk", "uly"), None),
        P(("blk", "uly"), None),
        P(("blk", "uly")),
        P(),
        P(),
        P(),
    )
    return jax.shard_map(
        body, mesh=mesh, in_specs=placed, out_specs=P(("blk", "uly"), None), check_vma=False
    )
```

```python
import functools
import math

import jax
import jax.numpy as jnp
import numpy as np
from jax import lax
from jax.experimental import pallas as pl
from jax.experimental.pallas import tpu as pltpu
from jax.sharding import PartitionSpec as P

HD = 128
ROPE_BASE = 500000.0
NX, NY, NZ = 4, 8, 4
CHIPS = NY * NZ
MESH = pl.DeviceIdType.MESH
NEAR = (0, 1, 7, 2, 6, 3, 5, 4)
FAR = NEAR[::-1]
KV_ORDER = sorted([(dy, dz) for dy in range(NY) for dz in range(NZ)], key=lambda d: (min(d[0], NY - d[0]) + d[1], d))
Q_ORDER = sorted([(dy, dz) for dy in range(NY) for dz in range(NZ)], key=lambda d: (min(d[0], NY - d[0]) + d[1], d))
SENDS = [("kv", dy, dz) for dy, dz in KV_ORDER] + [("q", dy, dz) for dy, dz in Q_ORDER]
SCALE = math.log2(math.e) / math.sqrt(HD)


def kernel(rows, q_hbm, k_hbm, v_hbm, flags_hbm, qm_hbm, km_hbm, vm_hbm, base_hbm, step_hbm, out_ref,
           q_in, k_in, v_in, flags_ref, qm_ref, km_ref, vm_ref, base_ref, step_ref, masks, kv_stage, q_stage, kv_buf, q_buf, o_stage,
           in_sem, kv_send, q_send, fwd_send, o_send, kv_recv, q_recv, fwd_recv, o_recv, ready):
    blk, uly = lax.axis_index("blk"), lax.axis_index("uly")
    blk0, y, z, core = blk // NY * NY, blk % NY, uly // 2, uly % 2
    here = y * NZ + z
    sibling = (blk, z * 2 + 1 - core)
    half = CHIPS * rows

    place = z * NY + y
    y_at = [y] + [jnp.where(y + d >= NY, y + d - NY, y + d) for d in range(1, NY)]
    z_at = [z, z + 1 - 2 * (z % 2), z + 2 - 4 * (z // 2), NZ - 1 - z]

    def turn_of(cy, cz):
        away = jnp.minimum(cy, NY - cy)
        late = jnp.where(cy + cz + blk0 + core == 0, 10, 0)
        return (z_step * cz + away + late) * CHIPS + cz * NY + cy

    far_half = blk0 // (NY * NX)
    z_step = 4 - 3 * far_half
    my_turn = turn_of(y, z)
    chips = [(cy, cz) for cz in range(NZ) for cy in range(NY)]
    turns = [turn_of(cy, cz) for cy, cz in chips]
    barrier = pltpu.get_barrier_semaphore()
    for (cy, cz), turn in zip(chips, turns):
        @pl.when(turn > my_turn)
        def _():
            pl.semaphore_signal(barrier, inc=1, device_id=(blk0 + cy, cz * 2 + core), device_id_type=MESH)

    @pl.when(core == 1)
    def _():
        pl.semaphore_signal(barrier, inc=1, device_id=sibling, device_id_type=MESH)

    loads = [
        pltpu.make_async_copy(src, dst, in_sem.at[i])
        for i, (src, dst) in enumerate((
            (base_hbm.at[y * (NZ * 2) + uly], base_ref), (step_hbm, step_ref), (flags_hbm, flags_ref), (qm_hbm, qm_ref), (km_hbm, km_ref), (vm_hbm, vm_ref),
            (k_hbm, k_in), (v_hbm, v_in), (q_hbm, q_in),
        ))
    ]
    for load in loads:
        load.start()

    entered = 1 - core
    for turn in turns:
        entered = entered + jnp.where(turn < my_turn, 1, 0)
    @pl.when(entered > 0)
    def _():
        pl.semaphore_wait(barrier, entered)

    for (cy, cz), turn in zip(chips, turns):
        @pl.when(turn < my_turn)
        def _():
            pl.semaphore_signal(ready.at[here], inc=1, device_id=(blk0 + cy, cz * 2 + core), device_id_type=MESH)

    @pl.when(core == 0)
    def _():
        pl.semaphore_signal(ready.at[here], inc=1, device_id=sibling, device_id_type=MESH)

    for load in loads[:6]:
        load.wait()

    lane = lax.broadcasted_iota(jnp.int32, (rows, HD), 1)
    turn, offset = base_ref[...], step_ref[...]
    cosine = turn[0:1] * offset[0] - turn[1:2] * offset[1]
    sine = turn[1:2] * offset[0] + turn[0:1] * offset[1]
    sine = jnp.where(lane < HD // 2, -sine, sine)
    diagonal = lax.broadcasted_iota(jnp.int32, (rows, rows), 0) == lax.broadcasted_iota(jnp.int32, (rows, rows), 1)
    flag_column = jnp.sum(
        jnp.where(diagonal, flags_ref[...].astype(jnp.float32), 0.0), axis=1, keepdims=True
    )
    masked = jnp.broadcast_to(flag_column, (rows, HD)) == 1.0

    for i, m_ref in enumerate((qm_ref, km_ref, vm_ref)):
        masks[i] = m_ref[...].astype(jnp.float32)

    def picked(x_in, which, chip):
        x = x_in[:, chip * HD:(chip + 1) * HD].astype(jnp.float32)
        return jnp.where(masked, masks[which, chip:chip + 1, :], x)

    def rotated(x):
        return (x * cosine + pltpu.roll(x, HD // 2, 1) * sine).astype(jnp.bfloat16)

    loads[6].wait()
    loads[7].wait()

    for chip in range(CHIPS):
        kv_stage[chip, 0] = rotated(picked(k_in, 1, chip))
        kv_stage[chip, 1] = picked(v_in, 2, chip).astype(jnp.bfloat16)
    loads[8].wait()
    for chip in range(CHIPS):
        q_stage[chip] = rotated(picked(q_in, 0, chip))

    def slot(i):
        return pl.ds(pl.multiple_of(i * rows, rows), rows)

    def peer(dy, dz):
        return y_at[dy] * NZ + z_at[dz], (blk0 + y_at[dy], z_at[dz] * 2 + core)

    def send_kv(dy, dz):
        chip, device = peer(dy, dz)
        pltpu.make_async_remote_copy(
            kv_stage.at[chip], kv_buf.at[:, slot(place)], kv_send, kv_recv.at[z],
            device_id=device, device_id_type=MESH,
        ).start()

    def send_q(dy, dz):
        chip, device = peer(dy, dz)
        if dy + dz:
            pltpu.make_async_remote_copy(
                q_stage.at[chip], q_buf.at[slot(place)], q_send, q_recv.at[z],
                device_id=device, device_id_type=MESH,
            ).start()
        else:
            pltpu.make_async_copy(q_stage.at[here], q_buf.at[slot(place)], q_recv.at[z]).start()

    pltpu.make_async_copy(kv_stage.at[here], kv_buf.at[:, slot(place)], kv_recv.at[z]).start()
    for dy, dz in KV_ORDER:
        @pl.when(turn_of(y_at[dy], z_at[dz]) < my_turn)
        def _():
            send_kv(dy, dz)

    for dy, dz in KV_ORDER:
        @pl.when(turn_of(y_at[dy], z_at[dz]) > my_turn)
        def _():
            pl.semaphore_wait(ready.at[peer(dy, dz)[0]], 1)
            send_kv(dy, dz)

    for dy, dz in Q_ORDER:
        send_q(dy, dz)

    def drain(ref, sem):
        pltpu.make_async_copy(ref, ref, sem).wait()

    group = NY * rows

    @pl.when(core == 1)
    def _():
        pl.semaphore_wait(ready.at[here], 1)

    for g in range(NZ):
        part = pl.ds(g * group, group)
        drain(kv_buf.at[:, part], kv_recv.at[g])
        pltpu.make_async_remote_copy(
            kv_buf.at[:, part], kv_buf.at[:, pl.ds(half + g * group, group)], fwd_send, fwd_recv,
            device_id=sibling, device_id_type=MESH,
        ).start()
    drain(kv_buf.at[:, pl.ds(half, half)], fwd_recv)

    column = pl.ds(pl.multiple_of(here * HD, HD), HD)
    spans = []
    for g in range(NZ):
        spans += [(g, 0, NY // 2), (g, NY // 2, NY)] if g == 0 else [(g, 0, NY)]
    for g, y_from, y_to in spans:
        if y_from == 0:
            drain(q_buf.at[pl.ds(g * group, group)], q_recv.at[g])
        part = pl.ds(g * group + y_from * rows, (y_to - y_from) * rows)
        scores = lax.dot_general(
            q_buf[part, :], kv_buf[0], (((1,), (1,)), ((), ())), preferred_element_type=jnp.float32
        )
        top = jnp.max(scores, axis=1, keepdims=True)
        weights = jnp.exp2((scores - top) * SCALE)
        total = jnp.sum(weights, axis=1, keepdims=True)
        mixture = jnp.dot(weights.astype(jnp.bfloat16), kv_buf[1], preferred_element_type=jnp.float32)
        o_stage[part, :] = (mixture / total).astype(jnp.bfloat16)
        for cy in range(y_from, y_to):
            source = pl.ds((g * NY + cy) * rows, rows)
            back = functools.partial(
                pltpu.make_async_remote_copy, o_stage.at[source], out_ref.at[:, column], o_send, o_recv,
                device_id=(blk0 + cy, g * 2 + core), device_id_type=MESH,
            )

            @pl.when(place != g * NY + cy)
            def _():
                back().start()

            @pl.when(place == g * NY + cy)
            def _():
                pltpu.make_async_copy(o_stage.at[source], out_ref.at[:, column], o_recv).start()

    others = CHIPS - 1
    drain(kv_stage.at[pl.ds(0, others)], kv_send)
    drain(q_stage.at[pl.ds(0, others)], q_send)
    drain(kv_buf.at[:, pl.ds(0, half)], fwd_send)
    drain(out_ref, o_recv)
    drain(o_stage.at[pl.ds(0, others * rows)], o_send)


def body(queries, keys, values, flags, q_mask, k_mask, v_mask):
    rows, width = queries.shape
    half = CHIPS * rows
    pair_lanes = np.arange(HD) % (HD // 2)
    freq = np.exp(pair_lanes * (-2.0 * math.log(ROPE_BASE) / HD)).astype(np.float32).astype(np.float64)
    base = np.arange(NY * NZ * 2)[:, None] * rows * freq
    step = np.arange(rows)[:, None] * freq
    base = np.stack([np.cos(base), np.sin(base)], axis=1).astype(np.float32)
    step = np.stack([np.cos(step), np.sin(step)]).astype(np.float32)
    vmem = pl.BlockSpec(memory_space=pltpu.VMEM)
    hbm = pl.BlockSpec(memory_space=pltpu.HBM)
    return pl.pallas_call(
        functools.partial(kernel, rows),
        out_shape=pltpu.VMEM((rows, width), jnp.bfloat16),
        in_specs=[hbm] * 9,
        out_specs=vmem,
        scratch_shapes=[
            pltpu.VMEM((rows, width), jnp.bfloat16),
            pltpu.VMEM((rows, width), jnp.bfloat16),
            pltpu.VMEM((rows, width), jnp.bfloat16),
            pltpu.VMEM((1, rows), jnp.int32),
            pltpu.VMEM((CHIPS, HD), jnp.bfloat16),
            pltpu.VMEM((CHIPS, HD), jnp.bfloat16),
            pltpu.VMEM((CHIPS, HD), jnp.bfloat16),
            pltpu.VMEM((2, HD), jnp.float32),
            pltpu.VMEM((2, rows, HD), jnp.float32),
            pltpu.VMEM((3, CHIPS, HD), jnp.float32),
            pltpu.VMEM((CHIPS, 2, rows, HD), jnp.bfloat16),
            pltpu.VMEM((CHIPS, rows, HD), jnp.bfloat16),
            pltpu.VMEM((2, 2 * half, HD), jnp.bfloat16),
            pltpu.VMEM((half, HD), jnp.bfloat16),
            pltpu.VMEM((half, HD), jnp.bfloat16),
            pltpu.SemaphoreType.DMA((9,)),
            pltpu.SemaphoreType.DMA,
            pltpu.SemaphoreType.DMA,
            pltpu.SemaphoreType.DMA,
            pltpu.SemaphoreType.DMA,
            pltpu.SemaphoreType.DMA((4,)),
            pltpu.SemaphoreType.DMA((4,)),
            pltpu.SemaphoreType.DMA,
            pltpu.SemaphoreType.DMA,
            pltpu.SemaphoreType.REGULAR((CHIPS,)),
        ],
        compiler_params=pltpu.CompilerParams(
            collective_id=0, has_side_effects=True, vmem_limit_bytes=48 * 2**20
        ),
        name="attend_plane",
    )(
        *(pltpu.with_memory_space_constraint(x, pltpu.HBM) for x in (
            queries, keys, values, flags.reshape(1, rows),
            q_mask.reshape(CHIPS, HD), k_mask.reshape(CHIPS, HD), v_mask.reshape(CHIPS, HD), jnp.asarray(base), jnp.asarray(step),
        ))
    )


def solution(mesh):
    placed = (
        P(("blk", "uly"), None),
        P(("blk", "uly"), None),
        P(("blk", "uly"), None),
        P(("blk", "uly")),
        P(),
        P(),
        P(),
    )
    return jax.shard_map(
        body, mesh=mesh, in_specs=placed, out_specs=P(("blk", "uly"), None), check_vma=False
    )
```

```python
import functools
import math

import jax
import jax.numpy as jnp
import numpy as np
from jax import lax
from jax.experimental import pallas as pl
from jax.experimental.pallas import tpu as pltpu
from jax.sharding import PartitionSpec as P

HD = 128
ROPE_BASE = 500000.0
NX, NY, NZ = 4, 8, 4
CHIPS = NY * NZ
MESH = pl.DeviceIdType.MESH
NEAR = (0, 1, 7, 2, 6, 3, 5, 4)
FAR = NEAR[::-1]
KV_ORDER = sorted([(dy, dz) for dy in range(NY) for dz in range(NZ)], key=lambda d: (min(d[0], NY - d[0]) + d[1], d))
Q_ORDER = [(0, 0), (2, 1), (3, 3), (2, 2), (0, 1), (7, 1), (7, 3), (5, 2), (1, 0), (6, 2), (2, 0), (6, 3), (5, 3), (4, 0), (5, 1), (6, 1), (4, 1), (4, 3), (7, 2), (3, 0), (4, 2), (3, 2), (2, 3), (1, 3), (3, 1), (1, 2), (1, 1), (0, 3), (6, 0), (7, 0), (0, 2), (5, 0)]
SENDS = [("kv", dy, dz) for dy, dz in KV_ORDER] + [("q", dy, dz) for dy, dz in Q_ORDER]
SCALE = math.log2(math.e) / math.sqrt(HD)


def kernel(rows, q_hbm, k_hbm, v_hbm, flags_hbm, qm_hbm, km_hbm, vm_hbm, base_hbm, step_hbm, out_ref,
           q_in, k_in, v_in, flags_ref, qm_ref, km_ref, vm_ref, base_ref, step_ref, masks, kv_stage, q_stage, kv_buf, q_buf, o_stage,
           in_sem, kv_send, q_send, fwd_send, o_send, kv_recv, q_recv, fwd_recv, o_recv, ready):
    blk, uly = lax.axis_index("blk"), lax.axis_index("uly")
    blk0, y, z, core = blk // NY * NY, blk % NY, uly // 2, uly % 2
    here = y * NZ + z
    sibling = (blk, z * 2 + 1 - core)
    half = CHIPS * rows

    place = z * NY + y
    y_at = [y] + [jnp.where(y + d >= NY, y + d - NY, y + d) for d in range(1, NY)]
    z_at = [z, z + 1 - 2 * (z % 2), z + 2 - 4 * (z // 2), NZ - 1 - z]

    def turn_of(cy, cz):
        away = jnp.minimum(cy, NY - cy)
        late = jnp.where(cy + cz + blk0 + core == 0, 12, 0)
        return (z_step * cz + away + late) * CHIPS + cz * NY + cy

    far_half = blk0 // (NY * NX)
    z_step = 2 - far_half
    my_turn = turn_of(y, z)
    chips = [(cy, cz) for cz in range(NZ) for cy in range(NY)]
    turns = [turn_of(cy, cz) for cy, cz in chips]
    barrier = pltpu.get_barrier_semaphore()
    for (cy, cz), turn in zip(chips, turns):
        @pl.when(turn > my_turn)
        def _():
            pl.semaphore_signal(barrier, inc=1, device_id=(blk0 + cy, cz * 2 + core), device_id_type=MESH)

    @pl.when(core == 1)
    def _():
        pl.semaphore_signal(barrier, inc=1, device_id=sibling, device_id_type=MESH)

    loads = [
        pltpu.make_async_copy(src, dst, in_sem.at[i])
        for i, (src, dst) in enumerate((
            (base_hbm.at[y * (NZ * 2) + uly], base_ref), (step_hbm, step_ref), (flags_hbm, flags_ref), (qm_hbm, qm_ref), (km_hbm, km_ref), (vm_hbm, vm_ref),
            (k_hbm, k_in), (v_hbm, v_in), (q_hbm, q_in),
        ))
    ]
    for load in loads:
        load.start()

    entered = 1 - core
    for turn in turns:
        entered = entered + jnp.where(turn < my_turn, 1, 0)
    @pl.when(entered > 0)
    def _():
        pl.semaphore_wait(barrier, entered)

    for (cy, cz), turn in zip(chips, turns):
        @pl.when(turn < my_turn)
        def _():
            pl.semaphore_signal(ready.at[here], inc=1, device_id=(blk0 + cy, cz * 2 + core), device_id_type=MESH)

    @pl.when(core == 0)
    def _():
        pl.semaphore_signal(ready.at[here], inc=1, device_id=sibling, device_id_type=MESH)

    for load in loads[:6]:
        load.wait()

    lane = lax.broadcasted_iota(jnp.int32, (rows, HD), 1)
    turn, offset = base_ref[...], step_ref[...]
    cosine = turn[0:1] * offset[0] - turn[1:2] * offset[1]
    sine = turn[1:2] * offset[0] + turn[0:1] * offset[1]
    sine = jnp.where(lane < HD // 2, -sine, sine)
    diagonal = lax.broadcasted_iota(jnp.int32, (rows, rows), 0) == lax.broadcasted_iota(jnp.int32, (rows, rows), 1)
    flag_column = jnp.sum(
        jnp.where(diagonal, flags_ref[...].astype(jnp.float32), 0.0), axis=1, keepdims=True
    )
    masked = jnp.broadcast_to(flag_column, (rows, HD)) == 1.0

    for i, m_ref in enumerate((qm_ref, km_ref, vm_ref)):
        masks[i] = m_ref[...].astype(jnp.float32)

    def picked(x_in, which, chip):
        x = x_in[:, chip * HD:(chip + 1) * HD].astype(jnp.float32)
        return jnp.where(masked, masks[which, chip:chip + 1, :], x)

    def rotated(x):
        return (x * cosine + pltpu.roll(x, HD // 2, 1) * sine).astype(jnp.bfloat16)

    loads[6].wait()
    loads[7].wait()

    for chip in range(CHIPS):
        kv_stage[chip, 0] = rotated(picked(k_in, 1, chip))
        kv_stage[chip, 1] = picked(v_in, 2, chip).astype(jnp.bfloat16)
    loads[8].wait()
    for chip in range(CHIPS):
        q_stage[chip] = rotated(picked(q_in, 0, chip))

    def slot(i):
        return pl.ds(pl.multiple_of(i * rows, rows), rows)

    def peer(dy, dz):
        return y_at[dy] * NZ + z_at[dz], (blk0 + y_at[dy], z_at[dz] * 2 + core)

    def send_kv(dy, dz):
        chip, device = peer(dy, dz)
        pltpu.make_async_remote_copy(
            kv_stage.at[chip], kv_buf.at[:, slot(place)], kv_send, kv_recv.at[z],
            device_id=device, device_id_type=MESH,
        ).start()

    def send_q(dy, dz):
        chip, device = peer(dy, dz)
        if dy + dz:
            pltpu.make_async_remote_copy(
                q_stage.at[chip], q_buf.at[slot(place)], q_send, q_recv.at[z],
                device_id=device, device_id_type=MESH,
            ).start()
        else:
            pltpu.make_async_copy(q_stage.at[here], q_buf.at[slot(place)], q_recv.at[z]).start()

    pltpu.make_async_copy(kv_stage.at[here], kv_buf.at[:, slot(place)], kv_recv.at[z]).start()
    for dy, dz in KV_ORDER:
        @pl.when(turn_of(y_at[dy], z_at[dz]) < my_turn)
        def _():
            send_kv(dy, dz)

    for dy, dz in KV_ORDER:
        @pl.when(turn_of(y_at[dy], z_at[dz]) > my_turn)
        def _():
            pl.semaphore_wait(ready.at[peer(dy, dz)[0]], 1)
            send_kv(dy, dz)

    for dy, dz in Q_ORDER:
        send_q(dy, dz)

    def drain(ref, sem):
        pltpu.make_async_copy(ref, ref, sem).wait()

    group = NY * rows

    @pl.when(core == 1)
    def _():
        pl.semaphore_wait(ready.at[here], 1)

    for g in range(NZ):
        part = pl.ds(g * group, group)
        drain(kv_buf.at[:, part], kv_recv.at[g])
        pltpu.make_async_remote_copy(
            kv_buf.at[:, part], kv_buf.at[:, pl.ds(half + g * group, group)], fwd_send, fwd_recv,
            device_id=sibling, device_id_type=MESH,
        ).start()
    drain(kv_buf.at[:, pl.ds(half, half)], fwd_recv)

    column = pl.ds(pl.multiple_of(here * HD, HD), HD)
    spans = []
    for g in range(NZ):
        spans += [(g, 0, NY // 2), (g, NY // 2, NY)] if g == 0 else [(g, 0, NY)]
    for g, y_from, y_to in spans:
        if y_from == 0:
            drain(q_buf.at[pl.ds(g * group, group)], q_recv.at[g])
        part = pl.ds(g * group + y_from * rows, (y_to - y_from) * rows)
        scores = lax.dot_general(
            q_buf[part, :], kv_buf[0], (((1,), (1,)), ((), ())), preferred_element_type=jnp.float32
        )
        top = jnp.max(scores, axis=1, keepdims=True)
        weights = jnp.exp2((scores - top) * SCALE)
        total = jnp.sum(weights, axis=1, keepdims=True)
        mixture = jnp.dot(weights.astype(jnp.bfloat16), kv_buf[1], preferred_element_type=jnp.float32)
        o_stage[part, :] = (mixture / total).astype(jnp.bfloat16)
        for cy in range(y_from, y_to):
            source = pl.ds((g * NY + cy) * rows, rows)
            back = functools.partial(
                pltpu.make_async_remote_copy, o_stage.at[source], out_ref.at[:, column], o_send, o_recv,
                device_id=(blk0 + cy, g * 2 + core), device_id_type=MESH,
            )

            @pl.when(place != g * NY + cy)
            def _():
                back().start()

            @pl.when(place == g * NY + cy)
            def _():
                pltpu.make_async_copy(o_stage.at[source], out_ref.at[:, column], o_recv).start()

    others = CHIPS - 1
    drain(kv_stage.at[pl.ds(0, others)], kv_send)
    drain(q_stage.at[pl.ds(0, others)], q_send)
    drain(kv_buf.at[:, pl.ds(0, half)], fwd_send)
    drain(out_ref, o_recv)
    drain(o_stage.at[pl.ds(0, others * rows)], o_send)


def body(queries, keys, values, flags, q_mask, k_mask, v_mask):
    rows, width = queries.shape
    half = CHIPS * rows
    pair_lanes = np.arange(HD) % (HD // 2)
    freq = np.exp(pair_lanes * (-2.0 * math.log(ROPE_BASE) / HD)).astype(np.float32).astype(np.float64)
    base = np.arange(NY * NZ * 2)[:, None] * rows * freq
    step = np.arange(rows)[:, None] * freq
    base = np.stack([np.cos(base), np.sin(base)], axis=1).astype(np.float32)
    step = np.stack([np.cos(step), np.sin(step)]).astype(np.float32)
    vmem = pl.BlockSpec(memory_space=pltpu.VMEM)
    hbm = pl.BlockSpec(memory_space=pltpu.HBM)
    return pl.pallas_call(
        functools.partial(kernel, rows),
        out_shape=pltpu.VMEM((rows, width), jnp.bfloat16),
        in_specs=[hbm] * 9,
        out_specs=vmem,
        scratch_shapes=[
            pltpu.VMEM((rows, width), jnp.bfloat16),
            pltpu.VMEM((rows, width), jnp.bfloat16),
            pltpu.VMEM((rows, width), jnp.bfloat16),
            pltpu.VMEM((1, rows), jnp.int32),
            pltpu.VMEM((CHIPS, HD), jnp.bfloat16),
            pltpu.VMEM((CHIPS, HD), jnp.bfloat16),
            pltpu.VMEM((CHIPS, HD), jnp.bfloat16),
            pltpu.VMEM((2, HD), jnp.float32),
            pltpu.VMEM((2, rows, HD), jnp.float32),
            pltpu.VMEM((3, CHIPS, HD), jnp.float32),
            pltpu.VMEM((CHIPS, 2, rows, HD), jnp.bfloat16),
            pltpu.VMEM((CHIPS, rows, HD), jnp.bfloat16),
            pltpu.VMEM((2, 2 * half, HD), jnp.bfloat16),
            pltpu.VMEM((half, HD), jnp.bfloat16),
            pltpu.VMEM((half, HD), jnp.bfloat16),
            pltpu.SemaphoreType.DMA((9,)),
            pltpu.SemaphoreType.DMA,
            pltpu.SemaphoreType.DMA,
            pltpu.SemaphoreType.DMA,
            pltpu.SemaphoreType.DMA,
            pltpu.SemaphoreType.DMA((4,)),
            pltpu.SemaphoreType.DMA((4,)),
            pltpu.SemaphoreType.DMA,
            pltpu.SemaphoreType.DMA,
            pltpu.SemaphoreType.REGULAR((CHIPS,)),
        ],
        compiler_params=pltpu.CompilerParams(
            collective_id=0, has_side_effects=True, vmem_limit_bytes=48 * 2**20
        ),
        name="attend_plane",
    )(
        *(pltpu.with_memory_space_constraint(x, pltpu.HBM) for x in (
            queries, keys, values, flags.reshape(1, rows),
            q_mask.reshape(CHIPS, HD), k_mask.reshape(CHIPS, HD), v_mask.reshape(CHIPS, HD), jnp.asarray(base), jnp.asarray(step),
        ))
    )


def solution(mesh):
    placed = (
        P(("blk", "uly"), None),
        P(("blk", "uly"), None),
        P(("blk", "uly"), None),
        P(("blk", "uly")),
        P(),
        P(),
        P(),
    )
    return jax.shard_map(
        body, mesh=mesh, in_specs=placed, out_specs=P(("blk", "uly"), None), check_vma=False
    )
```
